32 devices in a mesh: rep: 2 (over y), blk: 8 (over z, x), sub: 2 (over core).
Axes of the slice: x: 2, y: 2, z: 4, core: 2. Of those that a mesh axis runs over, the one named last changes fastest.
Arguments:
- queries: float32 [32, 4096], P(('rep', 'blk', 'sub')), parts along dimension 0, may hold values from -0.5 to 0.5
- passages: float32 [32, 4096], P(('rep', 'blk', 'sub')), parts along dimension 0, may hold values from -0.5 to 0.5
- positive: int32 [32], P(('rep', 'blk', 'sub')), parts along dimension 0, may hold values from 0 to 15, each once
Outputs:
- pair_loss: float32 [32], P(('rep', 'blk', 'sub')), parts along dimension 0
- grad_queries: float32 [32, 4096], P(('rep', 'blk', 'sub')), parts along dimension 0
- grad_passages: float32 [32, 4096], P(('rep', 'blk', 'sub')), parts along dimension 0
The draws below stay inside these ranges and needn't reach their ends.
There are 2 independent parts, one for each index of `rep`. The reference program is written for one: setup_inputs(seed, part) draws one part's arguments, and reference() takes and returns one part's arrays. A program takes and returns all parts, laid end to end along the dimension named above; each array names one. Nothing has to cross between parts.
All inputs are finite; a program needn't handle non-finite values.
Results may differ from the reference program's by a relative error of at most 0.0068.
Values may be sent and summed in bfloat16 or wider, within the bound.
A program may use at most 64 MiB of HBM per device.

```python
import math
import jax
import jax.numpy as jnp

D = 4096
PAIRS = 16


sigma_base = 0.0177


def passage_parts(key):
    noise = jax.random.truncated_normal(jax.random.fold_in(key, 11), -6.0, 6.0, (PAIRS, D), jnp.float32)
    spread = jnp.exp(jax.random.uniform(jax.random.fold_in(key, 12), (PAIRS, 1), jnp.float32, math.log(0.3), math.log(3.0)))
    twin_noise = jax.random.uniform(jax.random.fold_in(key, 13), (4, D), jnp.float32, -1.0, 1.0)
    common = jax.random.truncated_normal(jax.random.fold_in(key, 14), -6.0, 6.0, (1, D), jnp.float32)
    aligned = jax.random.uniform(jax.random.fold_in(key, 15), (8, D), jnp.float32, -1.0, 1.0)
    return (noise, spread, twin_noise, common, aligned)


def drawn_size():
    return math.sqrt(12.0 / D)


def build_passages(parts):
    noise, spread, twin_noise, common, aligned = parts
    edge = drawn_size()
    field = noise * spread * sigma_base
    field = field.at[0:8].set(aligned * edge)
    twins = 1.004 * field[0:8:2] + 0.05 * edge * twin_noise
    field = field.at[1:8:2].set(twins)
    return jnp.clip(field, -0.5, 0.5)


def draw_passages(key, part):
    parts = passage_parts(key)
    return build_passages(parts)


def build_queries(key, passages):
    noise = jax.random.truncated_normal(jax.random.fold_in(key, 21), -6.0, 6.0, (PAIRS, D), jnp.float32)
    spread = jnp.exp(jax.random.uniform(jax.random.fold_in(key, 22), (PAIRS, 1), jnp.float32, math.log(0.3), math.log(3.0)))
    field = noise * spread * sigma_base
    strengths = jnp.array([0.25, 0.6, 1.0, 1.6], jnp.float32)
    order = jax.random.permutation(jax.random.fold_in(key, 25), 4)
    factor = strengths[order][:, None]
    extra = jax.random.uniform(jax.random.fold_in(key, 23), (4, D), jnp.float32, -1.0, 1.0)
    own_noise = jax.random.uniform(jax.random.fold_in(key, 24), (4, D), jnp.float32, -1.0, 1.0)
    edge = drawn_size()
    lined = factor * passages[0:8:2]
    field = field.at[0:4].set(lined + 0.2 * edge * own_noise)
    field = field.at[4:8].set(1.004 * lined + 0.05 * edge * extra)
    return jnp.clip(field, -0.5, 0.5)


def draw_queries(key, part):
    parts = passage_parts(key)
    key = jax.random.fold_in(key, 5)
    return build_queries(key, build_passages(parts))


def setup_inputs(seed: int = 0, part: int = 0) -> dict:
    key_of = jax.random.split(jax.random.key(seed), 4)
    own_keys = jax.random.split(jax.random.fold_in(key_of[3], part), 4)
    return {
        "queries": draw_queries(jax.random.fold_in(jax.random.fold_in(key_of[3], part), 71), part),
        "passages": draw_passages(jax.random.fold_in(jax.random.fold_in(key_of[3], part), 71), part),
        "positive": jax.random.permutation(own_keys[2], PAIRS).astype(jnp.int32),
    }


score_scale = 50.0


def reference(queries, passages, positive):
    query_low = queries.astype(jnp.bfloat16)
    passage_low = passages.astype(jnp.bfloat16)
    scores = score_scale * jnp.dot(query_low, passage_low.T, preferred_element_type=jnp.float32)
    row_lse = jax.nn.logsumexp(scores, axis=1)
    col_lse = jax.nn.logsumexp(scores, axis=0)
    columns = jnp.arange(PAIRS, dtype=jnp.int32)
    mask = (positive[:, None] == columns[None, :]).astype(jnp.float32)
    pos_score = jnp.sum(scores * mask, axis=1)
    pair_loss = 0.5 * (row_lse + jnp.sum(mask * col_lse[None, :], axis=1)) - pos_score
    weights = 0.5 * (jnp.exp(scores - row_lse[:, None]) + jnp.exp(scores - col_lse[None, :])) - mask
    weights = weights.astype(jnp.bfloat16)
    grad_queries = score_scale * jnp.dot(weights, passage_low, preferred_element_type=jnp.float32)
    grad_passages = score_scale * jnp.dot(weights.T, query_low, preferred_element_type=jnp.float32)
    return pair_loss, grad_queries, grad_passages
```

```python
import functools

import jax
import jax.numpy as jnp
from jax import lax
from jax.experimental import pallas as pl
from jax.experimental.pallas import tpu as pltpu
from jax.sharding import PartitionSpec as P

score_scale = 50.0
MESH = pl.DeviceIdType.MESH
FOLD = 16


def merged(shard, axis, combine):
    everything = jax.tree.map(lambda part: lax.all_gather(part, axis), shard)
    first = jax.tree.map(lambda part: part[0], everything)

    def step(k, so_far):
        return combine(so_far, jax.tree.map(lambda part: part[k], everything))

    return lax.fori_loop(1, lax.axis_size(axis), step, first)


def against(left, right):
    return lax.dot_general(
        left, right, (((1,), (1,)), ((), ())), preferred_element_type=jnp.float32
    )


def combine_columns(earlier, later):
    top = jnp.maximum(earlier[0], later[0])
    total = earlier[1] * jnp.exp(earlier[0] - top) + later[1] * jnp.exp(later[0] - top)
    return (top, total)


def spread(queries, passages, positive):
    row_count = queries.shape[0]
    group = lax.axis_size("blk") * lax.axis_size("sub")
    pair_count = row_count * group
    start_row = lax.axis_index(("blk", "sub")) * row_count
    query_low = queries.astype(jnp.bfloat16)
    passage_low = passages.astype(jnp.bfloat16)
    all_pass = lax.all_gather(passage_low, ("blk", "sub"), axis=0, tiled=True)
    all_query, all_positive = (
        lax.all_gather(query_low, ("blk", "sub"), axis=0, tiled=True),
        lax.all_gather(positive, ("blk", "sub"), axis=0, tiled=True),
    )
    row_scores = score_scale * against(query_low, all_pass)
    columns = jnp.arange(pair_count, dtype=jnp.int32)
    row_mask = (positive[:, None] == columns[None, :]).astype(jnp.float32)
    row_top = jnp.max(row_scores, axis=1)
    row_lse = row_top + jnp.log(jnp.sum(jnp.exp(row_scores - row_top[:, None]), axis=1))
    pos_score = jnp.sum(row_scores * row_mask, axis=1)
    own_columns = start_row + jnp.arange(row_count, dtype=jnp.int32)
    col_mask = (all_positive[:, None] == own_columns[None, :]).astype(jnp.float32)
    part_top = jnp.max(row_scores, axis=0)
    part_total = jnp.sum(jnp.exp(row_scores - part_top[None, :]), axis=0)
    col_top, col_total = merged((part_top, part_total), ("blk", "sub"), combine_columns)
    col_lse_all = col_top + jnp.log(col_total)
    col_scores = score_scale * against(all_query, passage_low)
    all_row_lse = lax.all_gather(row_lse, ("blk", "sub"), axis=0, tiled=True)
    own_col_lse = lax.dynamic_slice_in_dim(col_lse_all, start_row, row_count, 0)
    pair_loss = 0.5 * (row_lse + jnp.sum(row_mask * col_lse_all[None, :], axis=1)) - pos_score
    row_weights = (
        0.5 * (jnp.exp(row_scores - row_lse[:, None]) + jnp.exp(row_scores - col_lse_all[None, :]))
        - row_mask
    )
    row_weights = row_weights.astype(jnp.bfloat16)
    grad_queries = score_scale * jnp.dot(row_weights, all_pass, preferred_element_type=jnp.float32)
    col_weights = (
        0.5
        * (jnp.exp(col_scores - all_row_lse[:, None]) + jnp.exp(col_scores - own_col_lse[None, :]))
        - col_mask
    )
    col_weights = col_weights.astype(jnp.bfloat16)
    grad_passages = score_scale * lax.dot_general(
        col_weights, all_query, (((0,), (0,)), ((), ())), preferred_element_type=jnp.float32
    )
    return (pair_loss, grad_queries, grad_passages)


def split3(x):
    high = x.astype(jnp.bfloat16)
    rest = x - high.astype(jnp.float32)
    mid = rest.astype(jnp.bfloat16)
    low = (rest - mid.astype(jnp.float32)).astype(jnp.bfloat16)
    return [high, mid, low]


def finish(pairs, me, both, pos, pos_of, loss_ref, grad_q_ref, grad_p_ref):
    width = both.shape[-1]
    flat = pairs * FOLD
    query = both[:, 0:FOLD, :].reshape(flat, width)
    passage = both[:, FOLD : 2 * FOLD, :].reshape(flat, width)

    row_of = lax.broadcasted_iota(jnp.int32, (flat, flat), 0)
    lane_of = lax.broadcasted_iota(jnp.int32, (flat, flat), 1)
    same_place = (row_of & (FOLD - 1)) == (lane_of & (FOLD - 1))
    block_ones = jnp.where(
        (row_of >> 4) == (lane_of >> 4), 1.0, 0.0
    ).astype(jnp.bfloat16)

    def folded(left, right):
        grid = jnp.where(same_place, against(left, right), 0.0)
        return jnp.sum(grid.reshape(pairs, FOLD, flat), axis=1)

    rows = split3(folded(query, passage))
    cols = split3(folded(passage, query))
    sums = jnp.dot(
        jnp.concatenate(rows + cols, axis=0), block_ones, preferred_element_type=jnp.float32
    )

    def part(k):
        return sums[k * pairs : (k + 1) * pairs]

    scores = score_scale * (part(0) + (part(1) + part(2)))
    scores_t = score_scale * (part(3) + (part(4) + part(5)))

    sub = lax.broadcasted_iota(jnp.int32, (pairs, flat), 0)
    own = sub == me

    def down(x):
        top = jnp.max(x, axis=0, keepdims=True)
        return top + jnp.log(jnp.sum(jnp.exp(x - top), axis=0, keepdims=True))

    def across(x):
        top = jnp.max(x, axis=1, keepdims=True)
        total = jnp.sum(jnp.exp(x - top), axis=1, keepdims=True) * (1.0 / FOLD)
        return top + jnp.log(total)

    col_lse_all = down(scores)
    row_lse_all = down(scores_t)
    row = jnp.sum(jnp.where(own, scores, 0.0), axis=0, keepdims=True)
    col = jnp.sum(jnp.where(own, scores_t, 0.0), axis=0, keepdims=True)
    row_lse = across(row)
    col_lse = across(col)

    lane = lax.broadcasted_iota(jnp.int32, (1, flat), 1)
    row_mask = (lane >> 4) == pos
    col_mask = pos_of == me.astype(jnp.float32)
    single = lane == pos * FOLD
    loss = 0.5 * row_lse + jnp.sum(
        jnp.where(single, 0.5 * col_lse_all - row, 0.0), axis=1, keepdims=True
    )
    loss_ref[...] = jnp.broadcast_to(loss, loss_ref.shape)

    row_w = 0.5 * (jnp.exp(row - row_lse) + jnp.exp(row - col_lse_all)) - jnp.where(row_mask, 1.0, 0.0)
    col_w = 0.5 * (jnp.exp(col - row_lse_all) + jnp.exp(col - col_lse)) - jnp.where(col_mask, 1.0, 0.0)

    place = lax.broadcasted_iota(jnp.int32, (FOLD, flat), 0) == (
        lax.broadcasted_iota(jnp.int32, (FOLD, flat), 1) & (FOLD - 1)
    )

    def grad(weights, rows, out_ref):
        wide = jnp.where(place, jnp.broadcast_to(weights, place.shape), 0.0).astype(jnp.bfloat16)
        result = score_scale * jnp.dot(wide, rows, preferred_element_type=jnp.float32)
        for c in range(FOLD):
            out_ref[0:1, c * width : (c + 1) * width] = result[c : c + 1, :]

    grad(row_w, passage, grad_q_ref)
    grad(col_w, query, grad_p_ref)


def kernel(
    subs, pairs,
    q_ref, p_ref, pos_ref,
    grad_q_ref, grad_p_ref, loss_ref,
    wide, both, places, send_sem, recv_sem, place_send, place_recv,
):
    width = both.shape[-1]
    me = lax.axis_index("blk") * subs + lax.axis_index("sub")

    def peer(k):
        other = lax.rem(me + k, pairs)
        return {"blk": other // subs, "sub": lax.rem(other, subs)}

    barrier = pltpu.get_barrier_semaphore()
    for k in range(1, pairs):
        pl.semaphore_signal(barrier, inc=1, device_id=peer(k), device_id_type=MESH)

    for c in range(FOLD):
        wide[c : c + 1, :] = q_ref[0:1, c * width : (c + 1) * width]
        wide[FOLD + c : FOLD + c + 1, :] = p_ref[0:1, c * width : (c + 1) * width]
    both[me] = wide[...].astype(jnp.bfloat16)
    pos = pos_ref[0]
    places[me] = jnp.full(places.shape[1:], pos.astype(jnp.float32), jnp.float32)

    pl.semaphore_wait(barrier, pairs - 1)
    copies = []
    for k in range(1, pairs):
        copies.append(
            pltpu.make_async_remote_copy(
                src_ref=places.at[me], dst_ref=places.at[me],
                send_sem=place_send.at[k], recv_sem=place_recv.at[k],
                device_id=peer(k), device_id_type=MESH,
            )
        )
        copies.append(
            pltpu.make_async_remote_copy(
                src_ref=both.at[me], dst_ref=both.at[me],
                send_sem=send_sem.at[k], recv_sem=recv_sem.at[k],
                device_id=peer(k), device_id_type=MESH,
            )
        )
        copies[-2].start()
        copies[-1].start()
    for copy in copies:
        copy.wait_recv()

    lane = lax.broadcasted_iota(jnp.int32, (1, pairs * FOLD), 1)
    pos_of = jnp.zeros((1, pairs * FOLD), jnp.float32)
    for k in range(pairs):
        pos_of = jnp.where((lane >> 4) == k, places[k, 0:1, :], pos_of)

    finish(pairs, me, both[...], pos, pos_of, loss_ref, grad_q_ref, grad_p_ref)
    for copy in copies:
        copy.wait_send()


def local(subs, pairs, queries, passages, positive):
    width = queries.shape[1] // FOLD
    vmem = pl.BlockSpec(memory_space=pltpu.VMEM)
    flat = pairs * FOLD
    grad_q, grad_p, loss = pl.pallas_call(
        functools.partial(kernel, subs, pairs),
        out_shape=(
            jax.ShapeDtypeStruct(queries.shape, jnp.float32),
            jax.ShapeDtypeStruct(passages.shape, jnp.float32),
            jax.ShapeDtypeStruct((1, 128), jnp.float32),
        ),
        in_specs=[vmem, vmem, pl.BlockSpec(memory_space=pltpu.SMEM)],
        out_specs=(vmem, vmem, vmem),
        scratch_shapes=[
            pltpu.VMEM((2 * FOLD, width), jnp.float32),
            pltpu.VMEM((pairs, 2 * FOLD, width), jnp.bfloat16),
            pltpu.VMEM((pairs, 1, flat), jnp.float32),
            pltpu.SemaphoreType.DMA((pairs,)),
            pltpu.SemaphoreType.DMA((pairs,)),
            pltpu.SemaphoreType.DMA((pairs,)),
            pltpu.SemaphoreType.DMA((pairs,)),
        ],
        compiler_params=pltpu.CompilerParams(collective_id=0, has_side_effects=True),
    )(queries, passages, positive)
    return loss[0, 0:1], grad_q, grad_p


def solution(mesh):
    in_specs = (
        P(("rep", "blk", "sub"), None),
        P(("rep", "blk", "sub"), None),
        P(("rep", "blk", "sub")),
    )
    out_specs = (
        P(("rep", "blk", "sub")),
        P(("rep", "blk", "sub"), None),
        P(("rep", "blk", "sub"), None),
    )
    subs = mesh.shape["sub"]
    group = mesh.shape["blk"] * subs

    def run(queries, passages, positive):
        if queries.shape[0] == 1 and group * FOLD <= 256:
            return local(subs, group, queries, passages, positive)
        return spread(queries, passages, positive)

    return jax.shard_map(run, mesh=mesh, in_specs=in_specs, out_specs=out_specs, check_vma=False)
```

```python
import functools

import jax
import jax.numpy as jnp
from jax import lax
from jax.experimental import pallas as pl
from jax.experimental.pallas import tpu as pltpu
from jax.sharding import PartitionSpec as P

score_scale = 50.0
MESH = pl.DeviceIdType.MESH
FOLD = 16


def merged(shard, axis, combine):
    everything = jax.tree.map(lambda part: lax.all_gather(part, axis), shard)
    first = jax.tree.map(lambda part: part[0], everything)

    def step(k, so_far):
        return combine(so_far, jax.tree.map(lambda part: part[k], everything))

    return lax.fori_loop(1, lax.axis_size(axis), step, first)


def against(left, right):
    return lax.dot_general(
        left, right, (((1,), (1,)), ((), ())), preferred_element_type=jnp.float32
    )


def combine_columns(earlier, later):
    top = jnp.maximum(earlier[0], later[0])
    total = earlier[1] * jnp.exp(earlier[0] - top) + later[1] * jnp.exp(later[0] - top)
    return (top, total)


def spread(queries, passages, positive):
    row_count = queries.shape[0]
    group = lax.axis_size("blk") * lax.axis_size("sub")
    pair_count = row_count * group
    start_row = lax.axis_index(("blk", "sub")) * row_count
    query_low = queries.astype(jnp.bfloat16)
    passage_low = passages.astype(jnp.bfloat16)
    all_pass = lax.all_gather(passage_low, ("blk", "sub"), axis=0, tiled=True)
    all_query, all_positive = (
        lax.all_gather(query_low, ("blk", "sub"), axis=0, tiled=True),
        lax.all_gather(positive, ("blk", "sub"), axis=0, tiled=True),
    )
    row_scores = score_scale * against(query_low, all_pass)
    columns = jnp.arange(pair_count, dtype=jnp.int32)
    row_mask = (positive[:, None] == columns[None, :]).astype(jnp.float32)
    row_top = jnp.max(row_scores, axis=1)
    row_lse = row_top + jnp.log(jnp.sum(jnp.exp(row_scores - row_top[:, None]), axis=1))
    pos_score = jnp.sum(row_scores * row_mask, axis=1)
    own_columns = start_row + jnp.arange(row_count, dtype=jnp.int32)
    col_mask = (all_positive[:, None] == own_columns[None, :]).astype(jnp.float32)
    part_top = jnp.max(row_scores, axis=0)
    part_total = jnp.sum(jnp.exp(row_scores - part_top[None, :]), axis=0)
    col_top, col_total = merged((part_top, part_total), ("blk", "sub"), combine_columns)
    col_lse_all = col_top + jnp.log(col_total)
    col_scores = score_scale * against(all_query, passage_low)
    all_row_lse = lax.all_gather(row_lse, ("blk", "sub"), axis=0, tiled=True)
    own_col_lse = lax.dynamic_slice_in_dim(col_lse_all, start_row, row_count, 0)
    pair_loss = 0.5 * (row_lse + jnp.sum(row_mask * col_lse_all[None, :], axis=1)) - pos_score
    row_weights = (
        0.5 * (jnp.exp(row_scores - row_lse[:, None]) + jnp.exp(row_scores - col_lse_all[None, :]))
        - row_mask
    )
    row_weights = row_weights.astype(jnp.bfloat16)
    grad_queries = score_scale * jnp.dot(row_weights, all_pass, preferred_element_type=jnp.float32)
    col_weights = (
        0.5
        * (jnp.exp(col_scores - all_row_lse[:, None]) + jnp.exp(col_scores - own_col_lse[None, :]))
        - col_mask
    )
    col_weights = col_weights.astype(jnp.bfloat16)
    grad_passages = score_scale * lax.dot_general(
        col_weights, all_query, (((0,), (0,)), ((), ())), preferred_element_type=jnp.float32
    )
    return (pair_loss, grad_queries, grad_passages)


def split3(x):
    high = x.astype(jnp.bfloat16)
    rest = x - high.astype(jnp.float32)
    mid = rest.astype(jnp.bfloat16)
    low = (rest - mid.astype(jnp.float32)).astype(jnp.bfloat16)
    return [high, mid, low]


def finish(pairs, me, both, pos, pos_of, loss_ref, grad_q_ref, grad_p_ref):
    width = both.shape[-1]
    flat = pairs * FOLD
    query = both[:, 0:FOLD, :].reshape(flat, width)
    passage = both[:, FOLD : 2 * FOLD, :].reshape(flat, width)

    row_of = lax.broadcasted_iota(jnp.int32, (flat, flat), 0)
    lane_of = lax.broadcasted_iota(jnp.int32, (flat, flat), 1)
    same_place = (row_of & (FOLD - 1)) == (lane_of & (FOLD - 1))
    block_ones = jnp.where(
        (row_of >> 4) == (lane_of >> 4), 1.0, 0.0
    ).astype(jnp.bfloat16)

    def folded(left, right):
        grid = jnp.where(same_place, against(left, right), 0.0)
        return jnp.sum(grid.reshape(pairs, FOLD, flat), axis=1)

    rows = split3(folded(query, passage))
    cols = split3(folded(passage, query))
    sums = jnp.dot(
        jnp.concatenate(rows + cols, axis=0), block_ones, preferred_element_type=jnp.float32
    )

    def part(k):
        return sums[k * pairs : (k + 1) * pairs]

    scores = score_scale * (part(0) + (part(1) + part(2)))
    scores_t = score_scale * (part(3) + (part(4) + part(5)))

    sub = lax.broadcasted_iota(jnp.int32, (pairs, flat), 0)
    own = sub == me

    def down(x):
        top = jnp.max(x, axis=0, keepdims=True)
        return top + jnp.log(jnp.sum(jnp.exp(x - top), axis=0, keepdims=True))

    def across(x):
        top = jnp.max(x, axis=1, keepdims=True)
        total = jnp.sum(jnp.exp(x - top), axis=1, keepdims=True) * (1.0 / FOLD)
        return top + jnp.log(total)

    col_lse_all = down(scores)
    row_lse_all = down(scores_t)
    row = jnp.sum(jnp.where(own, scores, 0.0), axis=0, keepdims=True)
    col = jnp.sum(jnp.where(own, scores_t, 0.0), axis=0, keepdims=True)
    row_lse = across(row)
    col_lse = across(col)

    lane = lax.broadcasted_iota(jnp.int32, (1, flat), 1)
    row_mask = (lane >> 4) == pos
    col_mask = pos_of == me.astype(jnp.float32)
    single = lane == pos * FOLD
    loss = 0.5 * row_lse + jnp.sum(
        jnp.where(single, 0.5 * col_lse_all - row, 0.0), axis=1, keepdims=True
    )
    loss_ref[...] = jnp.broadcast_to(loss, loss_ref.shape)

    row_w = 0.5 * (jnp.exp(row - row_lse) + jnp.exp(row - col_lse_all)) - jnp.where(row_mask, 1.0, 0.0)
    col_w = 0.5 * (jnp.exp(col - row_lse_all) + jnp.exp(col - col_lse)) - jnp.where(col_mask, 1.0, 0.0)

    place = lax.broadcasted_iota(jnp.int32, (FOLD, flat), 0) == (
        lax.broadcasted_iota(jnp.int32, (FOLD, flat), 1) & (FOLD - 1)
    )

    def grad(weights, rows, out_ref):
        wide = jnp.where(place, jnp.broadcast_to(weights, place.shape), 0.0).astype(jnp.bfloat16)
        result = jnp.dot(wide, rows, preferred_element_type=jnp.float32)
        for c in range(FOLD):
            out_ref[0:1, c * width : (c + 1) * width] = result[c : c + 1, :]

    grad(row_w, passage, grad_q_ref)
    grad(col_w, query, grad_p_ref)


def kernel(
    subs, pairs,
    q_ref, p_ref, pos_ref,
    grad_q_ref, grad_p_ref, loss_ref,
    wide, both, places, send_sem, recv_sem, place_send, place_recv,
):
    width = both.shape[-1]
    chips = pairs // subs
    chip, sub = lax.axis_index("blk"), lax.axis_index("sub")
    me = chip * subs + sub
    other = (subs - 1) - sub

    def rows_to(target, source, k):
        return (
            pltpu.make_async_remote_copy(
                src_ref=both.at[source], dst_ref=both.at[source],
                send_sem=send_sem.at[k], recv_sem=recv_sem.at[source],
                device_id=target, device_id_type=MESH,
            ),
            pltpu.make_async_remote_copy(
                src_ref=places.at[source], dst_ref=places.at[source],
                send_sem=place_send.at[k], recv_sem=place_recv.at[source],
                device_id=target, device_id_type=MESH,
            ),
        )

    def over_link(k, source):
        return rows_to({"blk": k, "sub": sub}, source, k)

    def across(k):
        return rows_to({"blk": chip, "sub": other}, k * subs + sub, chips + k)

    def start(copies):
        for copy in copies:
            copy.start()

    def wait_recv(copies):
        for copy in copies:
            copy.wait_recv()

    def wait_send(copies):
        for copy in copies:
            copy.wait_send()

    def each(first, end, body):
        def step(k, carry):
            body(k)
            return carry

        lax.fori_loop(first, end, step, 0)

    barrier = pltpu.get_barrier_semaphore()

    def greet(k):
        pl.semaphore_signal(
            barrier, inc=1, device_id={"blk": k, "sub": sub}, device_id_type=MESH
        )

    each(chip + 1, chips, greet)
    pl.semaphore_signal(
        barrier, inc=1, device_id={"blk": chip, "sub": other}, device_id_type=MESH
    )

    for c in range(FOLD):
        wide[c : c + 1, :] = q_ref[0:1, c * width : (c + 1) * width]
        wide[FOLD + c : FOLD + c + 1, :] = p_ref[0:1, c * width : (c + 1) * width]
    both[me] = wide[...].astype(jnp.bfloat16)
    pos = pos_ref[0]
    places[me] = jnp.full(places.shape[1:], pos.astype(jnp.float32), jnp.float32)

    pl.semaphore_wait(barrier, chip + 1)

    def send(k):
        start(over_link(k, me))

    def hand_on(k):
        wait_recv(over_link(k, k * subs + sub))
        start(across(k))

    def answer(k):
        hand_on(k)
        send(k)

    def receive(k):
        wait_recv(rows_to({"blk": chip, "sub": other}, k * subs + other, chips + k))

    each(0, chip, send)
    start(across(chip))
    each(chip + 1, chips, answer)
    each(0, chip, hand_on)
    each(0, chips, receive)

    lane = lax.broadcasted_iota(jnp.int32, (1, pairs * FOLD), 1)
    pos_of = jnp.zeros((1, pairs * FOLD), jnp.float32)
    for k in range(pairs):
        pos_of = jnp.where((lane >> 4) == k, places[k, 0:1, :], pos_of)

    finish(pairs, me, both[...], pos, pos_of, loss_ref, grad_q_ref, grad_p_ref)

    each(0, chip, lambda k: wait_send(over_link(k, me)))
    each(chip + 1, chips, lambda k: wait_send(over_link(k, me)))
    each(0, chips, lambda k: wait_send(across(k)))


def local(subs, pairs, queries, passages, positive):
    width = queries.shape[1] // FOLD
    vmem = pl.BlockSpec(memory_space=pltpu.VMEM)
    flat = pairs * FOLD
    grad_q, grad_p, loss = pl.pallas_call(
        functools.partial(kernel, subs, pairs),
        out_shape=(
            jax.ShapeDtypeStruct(queries.shape, jnp.float32),
            jax.ShapeDtypeStruct(passages.shape, jnp.float32),
            jax.ShapeDtypeStruct((1, 128), jnp.float32),
        ),
        in_specs=[vmem, vmem, pl.BlockSpec(memory_space=pltpu.SMEM)],
        out_specs=(vmem, vmem, vmem),
        scratch_shapes=[
            pltpu.VMEM((2 * FOLD, width), jnp.float32),
            pltpu.VMEM((pairs, 2 * FOLD, width), jnp.bfloat16),
            pltpu.VMEM((pairs, 1, flat), jnp.float32),
            pltpu.SemaphoreType.DMA((pairs,)),
            pltpu.SemaphoreType.DMA((pairs,)),
            pltpu.SemaphoreType.DMA((pairs,)),
            pltpu.SemaphoreType.DMA((pairs,)),
        ],
        compiler_params=pltpu.CompilerParams(collective_id=0, has_side_effects=True, vmem_limit_bytes=8 * 1024 * 1024),
    )(queries, passages, positive)
    return loss[0, 0:1], score_scale * grad_q, score_scale * grad_p


def solution(mesh):
    in_specs = (
        P(("rep", "blk", "sub"), None),
        P(("rep", "blk", "sub"), None),
        P(("rep", "blk", "sub")),
    )
    out_specs = (
        P(("rep", "blk", "sub")),
        P(("rep", "blk", "sub"), None),
        P(("rep", "blk", "sub"), None),
    )
    subs = mesh.shape["sub"]
    group = mesh.shape["blk"] * subs

    def run(queries, passages, positive):
        if queries.shape[0] == 1 and subs == 2 and group * FOLD <= 256:
            return local(subs, group, queries, passages, positive)
        return spread(queries, passages, positive)

    return jax.shard_map(run, mesh=mesh, in_specs=in_specs, out_specs=out_specs, check_vma=False)
```

```python
import functools

import jax
import jax.numpy as jnp
from jax import lax
from jax.experimental import pallas as pl
from jax.experimental.pallas import tpu as pltpu
from jax.sharding import PartitionSpec as P

score_scale = 50.0
MESH = pl.DeviceIdType.MESH
FOLD = 16


def merged(shard, axis, combine):
    everything = jax.tree.map(lambda part: lax.all_gather(part, axis), shard)
    first = jax.tree.map(lambda part: part[0], everything)

    def step(k, so_far):
        return combine(so_far, jax.tree.map(lambda part: part[k], everything))

    return lax.fori_loop(1, lax.axis_size(axis), step, first)


def against(left, right):
    return lax.dot_general(
        left, right, (((1,), (1,)), ((), ())), preferred_element_type=jnp.float32
    )


def combine_columns(earlier, later):
    top = jnp.maximum(earlier[0], later[0])
    total = earlier[1] * jnp.exp(earlier[0] - top) + later[1] * jnp.exp(later[0] - top)
    return (top, total)


def spread(queries, passages, positive):
    row_count = queries.shape[0]
    group = lax.axis_size("blk") * lax.axis_size("sub")
    pair_count = row_count * group
    start_row = lax.axis_index(("blk", "sub")) * row_count
    query_low = queries.astype(jnp.bfloat16)
    passage_low = passages.astype(jnp.bfloat16)
    all_pass = lax.all_gather(passage_low, ("blk", "sub"), axis=0, tiled=True)
    all_query, all_positive = (
        lax.all_gather(query_low, ("blk", "sub"), axis=0, tiled=True),
        lax.all_gather(positive, ("blk", "sub"), axis=0, tiled=True),
    )
    row_scores = score_scale * against(query_low, all_pass)
    columns = jnp.arange(pair_count, dtype=jnp.int32)
    row_mask = (positive[:, None] == columns[None, :]).astype(jnp.float32)
    row_top = jnp.max(row_scores, axis=1)
    row_lse = row_top + jnp.log(jnp.sum(jnp.exp(row_scores - row_top[:, None]), axis=1))
    pos_score = jnp.sum(row_scores * row_mask, axis=1)
    own_columns = start_row + jnp.arange(row_count, dtype=jnp.int32)
    col_mask = (all_positive[:, None] == own_columns[None, :]).astype(jnp.float32)
    part_top = jnp.max(row_scores, axis=0)
    part_total = jnp.sum(jnp.exp(row_scores - part_top[None, :]), axis=0)
    col_top, col_total = merged((part_top, part_total), ("blk", "sub"), combine_columns)
    col_lse_all = col_top + jnp.log(col_total)
    col_scores = score_scale * against(all_query, passage_low)
    all_row_lse = lax.all_gather(row_lse, ("blk", "sub"), axis=0, tiled=True)
    own_col_lse = lax.dynamic_slice_in_dim(col_lse_all, start_row, row_count, 0)
    pair_loss = 0.5 * (row_lse + jnp.sum(row_mask * col_lse_all[None, :], axis=1)) - pos_score
    row_weights = (
        0.5 * (jnp.exp(row_scores - row_lse[:, None]) + jnp.exp(row_scores - col_lse_all[None, :]))
        - row_mask
    )
    row_weights = row_weights.astype(jnp.bfloat16)
    grad_queries = score_scale * jnp.dot(row_weights, all_pass, preferred_element_type=jnp.float32)
    col_weights = (
        0.5
        * (jnp.exp(col_scores - all_row_lse[:, None]) + jnp.exp(col_scores - own_col_lse[None, :]))
        - col_mask
    )
    col_weights = col_weights.astype(jnp.bfloat16)
    grad_passages = score_scale * lax.dot_general(
        col_weights, all_query, (((0,), (0,)), ((), ())), preferred_element_type=jnp.float32
    )
    return (pair_loss, grad_queries, grad_passages)


def split3(x):
    high = x.astype(jnp.bfloat16)
    rest = x - high.astype(jnp.float32)
    mid = rest.astype(jnp.bfloat16)
    low = (rest - mid.astype(jnp.float32)).astype(jnp.bfloat16)
    return [high, mid, low]


def finish(pairs, me, both, pos, pos_of, loss_ref, grad_q_ref, grad_p_ref):
    width = both.shape[-1]
    flat = pairs * FOLD
    query = both[:, 0:FOLD, :].reshape(flat, width)
    passage = both[:, FOLD : 2 * FOLD, :].reshape(flat, width)

    row_of = lax.broadcasted_iota(jnp.int32, (flat, flat), 0)
    lane_of = lax.broadcasted_iota(jnp.int32, (flat, flat), 1)
    same_place = (row_of & (FOLD - 1)) == (lane_of & (FOLD - 1))
    block_ones = jnp.where(
        (row_of >> 4) == (lane_of >> 4), 1.0, 0.0
    ).astype(jnp.bfloat16)

    def folded(left, right):
        grid = jnp.where(same_place, against(left, right), 0.0)
        return jnp.sum(grid.reshape(pairs, FOLD, flat), axis=1)

    rows = split3(folded(query, passage))
    cols = split3(folded(passage, query))
    sums = jnp.dot(
        jnp.concatenate(rows + cols, axis=0), block_ones, preferred_element_type=jnp.float32
    )

    def part(k):
        return sums[k * pairs : (k + 1) * pairs]

    scores = score_scale * (part(0) + (part(1) + part(2)))
    scores_t = score_scale * (part(3) + (part(4) + part(5)))

    sub = lax.broadcasted_iota(jnp.int32, (pairs, flat), 0)
    own = sub == me

    def down(x):
        top = jnp.max(x, axis=0, keepdims=True)
        return top + jnp.log(jnp.sum(jnp.exp(x - top), axis=0, keepdims=True))

    def across(x):
        top = jnp.max(x, axis=1, keepdims=True)
        total = jnp.sum(jnp.exp(x - top), axis=1, keepdims=True) * (1.0 / FOLD)
        return top + jnp.log(total)

    col_lse_all = down(scores)
    row_lse_all = down(scores_t)
    row = jnp.sum(jnp.where(own, scores, 0.0), axis=0, keepdims=True)
    col = jnp.sum(jnp.where(own, scores_t, 0.0), axis=0, keepdims=True)
    row_lse = across(row)
    col_lse = across(col)

    lane = lax.broadcasted_iota(jnp.int32, (1, flat), 1)
    row_mask = (lane >> 4) == pos
    col_mask = pos_of == me.astype(jnp.float32)
    single = lane == pos * FOLD
    loss = 0.5 * row_lse + jnp.sum(
        jnp.where(single, 0.5 * col_lse_all - row, 0.0), axis=1, keepdims=True
    )
    loss_ref[...] = jnp.broadcast_to(loss, loss_ref.shape)

    row_w = 0.5 * (jnp.exp(row - row_lse) + jnp.exp(row - col_lse_all)) - jnp.where(row_mask, 1.0, 0.0)
    col_w = 0.5 * (jnp.exp(col - row_lse_all) + jnp.exp(col - col_lse)) - jnp.where(col_mask, 1.0, 0.0)

    place = lax.broadcasted_iota(jnp.int32, (FOLD, flat), 0) == (
        lax.broadcasted_iota(jnp.int32, (FOLD, flat), 1) & (FOLD - 1)
    )

    def grad(weights, rows, out_ref):
        wide = jnp.where(place, jnp.broadcast_to(weights, place.shape), 0.0).astype(jnp.bfloat16)
        result = jnp.dot(wide, rows, preferred_element_type=jnp.float32)
        for c in range(FOLD):
            out_ref[0:1, c * width : (c + 1) * width] = result[c : c + 1, :]

    grad(row_w, passage, grad_q_ref)
    grad(col_w, query, grad_p_ref)


def kernel(
    subs, pairs,
    q_hbm, p_hbm, pos_hbm,
    grad_q_ref, grad_p_ref, loss_ref,
    q_ref, p_ref, pos_ref, load_sem, ready, wide, both, places, send_sem, recv_sem, place_send, place_recv,
):
    width = both.shape[-1]
    chips = pairs // subs
    chip, sub = lax.axis_index("blk"), lax.axis_index("sub")
    me = chip * subs + sub
    other = (subs - 1) - sub

    def rows_to(target, source, k):
        return (
            pltpu.make_async_remote_copy(
                src_ref=both.at[source], dst_ref=both.at[source],
                send_sem=send_sem.at[k], recv_sem=recv_sem.at[source],
                device_id=target, device_id_type=MESH,
            ),
            pltpu.make_async_remote_copy(
                src_ref=places.at[source], dst_ref=places.at[source],
                send_sem=place_send.at[k], recv_sem=place_recv.at[source],
                device_id=target, device_id_type=MESH,
            ),
        )

    def over_link(k, source):
        return rows_to({"blk": k, "sub": sub}, source, k)

    def across(k):
        return rows_to({"blk": chip, "sub": other}, k * subs + sub, chips + k)

    def start(copies):
        for copy in copies:
            copy.start()

    def wait_recv(copies):
        for copy in copies:
            copy.wait_recv()

    def wait_send(copies):
        for copy in copies:
            copy.wait_send()

    def each(first, end, body):
        def step(k, carry):
            body(k)
            return carry

        lax.fori_loop(first, end, step, 0)

    barrier = pltpu.get_barrier_semaphore()

    def greet(k):
        pl.semaphore_signal(
            barrier, inc=1, device_id={"blk": k, "sub": sub}, device_id_type=MESH
        )

    each(chip + 1, chips, greet)
    pl.semaphore_signal(
        barrier, inc=1, device_id={"blk": chip, "sub": other}, device_id_type=MESH
    )
    q_copy = pltpu.make_async_copy(q_hbm, q_ref, load_sem.at[0])
    p_copy = pltpu.make_async_copy(p_hbm, p_ref, load_sem.at[1])
    pos_copy = pltpu.make_async_copy(pos_hbm, pos_ref, load_sem.at[2])
    pos_copy.start()
    q_copy.start()
    p_copy.start()

    pl.semaphore_wait(barrier, chip + 1)

    def tell(k):
        pl.semaphore_signal(
            ready.at[chip], inc=1, device_id={"blk": k, "sub": sub}, device_id_type=MESH
        )

    each(0, chip, tell)
    pos_copy.wait()
    pos = pos_ref[0]
    places[me] = jnp.full(places.shape[1:], pos.astype(jnp.float32), jnp.float32)
    q_copy.wait()
    p_copy.wait()
    for c in range(FOLD):
        wide[c : c + 1, :] = q_ref[0:1, c * width : (c + 1) * width]
        wide[FOLD + c : FOLD + c + 1, :] = p_ref[0:1, c * width : (c + 1) * width]
    both[me] = wide[...].astype(jnp.bfloat16)

    def send(k):
        start(over_link(k, me))

    def hand_on(k):
        wait_recv(over_link(k, k * subs + sub))
        start(across(k))

    def answer(k):
        pl.semaphore_wait(ready.at[k], 1)
        send(k)

    def receive(k):
        wait_recv(rows_to({"blk": chip, "sub": other}, k * subs + other, chips + k))

    each(0, chip, send)
    start(across(chip))
    each(chip + 1, chips, answer)
    each(chip + 1, chips, hand_on)
    each(0, chip, hand_on)
    each(0, chips, receive)

    lane = lax.broadcasted_iota(jnp.int32, (1, pairs * FOLD), 1)
    pos_of = jnp.zeros((1, pairs * FOLD), jnp.float32)
    for k in range(pairs):
        pos_of = jnp.where((lane >> 4) == k, places[k, 0:1, :], pos_of)

    finish(pairs, me, both[...], pos, pos_of, loss_ref, grad_q_ref, grad_p_ref)

    each(0, chip, lambda k: wait_send(over_link(k, me)))
    each(chip + 1, chips, lambda k: wait_send(over_link(k, me)))
    each(0, chips, lambda k: wait_send(across(k)))


def write_out(loss_ref, q_ref, p_ref, loss_out, q_out, p_out):
    loss_out[...] = loss_ref[0, 0:1]
    q_out[...] = score_scale * q_ref[...]
    p_out[...] = score_scale * p_ref[...]


def local(subs, pairs, queries, passages, positive):
    width = queries.shape[1] // FOLD
    vmem = pl.BlockSpec(memory_space=pltpu.VMEM)
    anywhere = pl.BlockSpec(memory_space=pltpu.HBM)
    flat = pairs * FOLD
    grad_q, grad_p, loss = pl.pallas_call(
        functools.partial(kernel, subs, pairs),
        out_shape=(
            pltpu.VMEM(queries.shape, jnp.float32),
            pltpu.VMEM(passages.shape, jnp.float32),
            pltpu.VMEM((1, 128), jnp.float32),
        ),
        in_specs=[anywhere, anywhere, anywhere],
        out_specs=(vmem, vmem, vmem),
        scratch_shapes=[
            pltpu.VMEM(queries.shape, jnp.float32),
            pltpu.VMEM(passages.shape, jnp.float32),
            pltpu.SMEM((1,), jnp.int32),
            pltpu.SemaphoreType.DMA((3,)),
            pltpu.SemaphoreType.REGULAR((pairs // subs,)),
            pltpu.VMEM((2 * FOLD, width), jnp.float32),
            pltpu.VMEM((pairs, 2 * FOLD, width), jnp.bfloat16),
            pltpu.VMEM((pairs, 1, flat), jnp.float32),
            pltpu.SemaphoreType.DMA((pairs,)),
            pltpu.SemaphoreType.DMA((pairs,)),
            pltpu.SemaphoreType.DMA((pairs,)),
            pltpu.SemaphoreType.DMA((pairs,)),
        ],
        compiler_params=pltpu.CompilerParams(collective_id=0, has_side_effects=True, vmem_limit_bytes=8 * 1024 * 1024),
    )(*(pltpu.with_memory_space_constraint(x, pltpu.HBM) for x in (queries, passages)), positive)
    return pl.pallas_call(
        write_out,
        out_shape=(
            jax.ShapeDtypeStruct((1,), jnp.float32),
            jax.ShapeDtypeStruct(queries.shape, jnp.float32),
            jax.ShapeDtypeStruct(passages.shape, jnp.float32),
        ),
        in_specs=[vmem, vmem, vmem],
        out_specs=(vmem, vmem, vmem),
        compiler_params=pltpu.CompilerParams(vmem_limit_bytes=8 * 1024 * 1024),
    )(loss, grad_q, grad_p)


def solution(mesh):
    in_specs = (
        P(("rep", "blk", "sub"), None),
        P(("rep", "blk", "sub"), None),
        P(("rep", "blk", "sub")),
    )
    out_specs = (
        P(("rep", "blk", "sub")),
        P(("rep", "blk", "sub"), None),
        P(("rep", "blk", "sub"), None),
    )
    subs = mesh.shape["sub"]
    group = mesh.shape["blk"] * subs

    def run(queries, passages, positive):
        if queries.shape[0] == 1 and subs == 2 and group * FOLD <= 256:
            return local(subs, group, queries, passages, positive)
        return spread(queries, passages, positive)

    return jax.shard_map(run, mesh=mesh, in_specs=in_specs, out_specs=out_specs, check_vma=False)
```

```python
import functools

import jax
import jax.numpy as jnp
from jax import lax
from jax.experimental import pallas as pl
from jax.experimental.pallas import tpu as pltpu
from jax.sharding import PartitionSpec as P

score_scale = 50.0
MESH = pl.DeviceIdType.MESH
FOLD = 16


def merged(shard, axis, combine):
    everything = jax.tree.map(lambda part: lax.all_gather(part, axis), shard)
    first = jax.tree.map(lambda part: part[0], everything)

    def step(k, so_far):
        return combine(so_far, jax.tree.map(lambda part: part[k], everything))

    return lax.fori_loop(1, lax.axis_size(axis), step, first)


def against(left, right):
    return lax.dot_general(
        left, right, (((1,), (1,)), ((), ())), preferred_element_type=jnp.float32
    )


def combine_columns(earlier, later):
    top = jnp.maximum(earlier[0], later[0])
    total = earlier[1] * jnp.exp(earlier[0] - top) + later[1] * jnp.exp(later[0] - top)
    return (top, total)


def spread(queries, passages, positive):
    row_count = queries.shape[0]
    group = lax.axis_size("blk") * lax.axis_size("sub")
    pair_count = row_count * group
    start_row = lax.axis_index(("blk", "sub")) * row_count
    query_low = queries.astype(jnp.bfloat16)
    passage_low = passages.astype(jnp.bfloat16)
    all_pass = lax.all_gather(passage_low, ("blk", "sub"), axis=0, tiled=True)
    all_query, all_positive = (
        lax.all_gather(query_low, ("blk", "sub"), axis=0, tiled=True),
        lax.all_gather(positive, ("blk", "sub"), axis=0, tiled=True),
    )
    row_scores = score_scale * against(query_low, all_pass)
    columns = jnp.arange(pair_count, dtype=jnp.int32)
    row_mask = (positive[:, None] == columns[None, :]).astype(jnp.float32)
    row_top = jnp.max(row_scores, axis=1)
    row_lse = row_top + jnp.log(jnp.sum(jnp.exp(row_scores - row_top[:, None]), axis=1))
    pos_score = jnp.sum(row_scores * row_mask, axis=1)
    own_columns = start_row + jnp.arange(row_count, dtype=jnp.int32)
    col_mask = (all_positive[:, None] == own_columns[None, :]).astype(jnp.float32)
    part_top = jnp.max(row_scores, axis=0)
    part_total = jnp.sum(jnp.exp(row_scores - part_top[None, :]), axis=0)
    col_top, col_total = merged((part_top, part_total), ("blk", "sub"), combine_columns)
    col_lse_all = col_top + jnp.log(col_total)
    col_scores = score_scale * against(all_query, passage_low)
    all_row_lse = lax.all_gather(row_lse, ("blk", "sub"), axis=0, tiled=True)
    own_col_lse = lax.dynamic_slice_in_dim(col_lse_all, start_row, row_count, 0)
    pair_loss = 0.5 * (row_lse + jnp.sum(row_mask * col_lse_all[None, :], axis=1)) - pos_score
    row_weights = (
        0.5 * (jnp.exp(row_scores - row_lse[:, None]) + jnp.exp(row_scores - col_lse_all[None, :]))
        - row_mask
    )
    row_weights = row_weights.astype(jnp.bfloat16)
    grad_queries = score_scale * jnp.dot(row_weights, all_pass, preferred_element_type=jnp.float32)
    col_weights = (
        0.5
        * (jnp.exp(col_scores - all_row_lse[:, None]) + jnp.exp(col_scores - own_col_lse[None, :]))
        - col_mask
    )
    col_weights = col_weights.astype(jnp.bfloat16)
    grad_passages = score_scale * lax.dot_general(
        col_weights, all_query, (((0,), (0,)), ((), ())), preferred_element_type=jnp.float32
    )
    return (pair_loss, grad_queries, grad_passages)


def split3(x):
    high = x.astype(jnp.bfloat16)
    rest = x - high.astype(jnp.float32)
    mid = rest.astype(jnp.bfloat16)
    low = (rest - mid.astype(jnp.float32)).astype(jnp.bfloat16)
    return [high, mid, low]


def finish(pairs, me, same_place, block_ones, both, pos, pos_of, loss_ref, grad_q_ref, grad_p_ref):
    width = both.shape[-1]
    flat = pairs * FOLD
    query = both[:, 0:FOLD, :].reshape(flat, width)
    passage = both[:, FOLD : 2 * FOLD, :].reshape(flat, width)

    def folded(left, right):
        grid = against(left, right) * same_place[...]
        return jnp.sum(grid.reshape(pairs, FOLD, flat), axis=1)

    rows = split3(folded(query, passage))
    cols = split3(folded(passage, query))
    sums = jnp.dot(
        jnp.concatenate(rows + cols, axis=0), block_ones[...], preferred_element_type=jnp.float32
    )

    def part(k):
        return sums[k * pairs : (k + 1) * pairs]

    scores = score_scale * (part(0) + (part(1) + part(2)))
    scores_t = score_scale * (part(3) + (part(4) + part(5)))

    sub = lax.broadcasted_iota(jnp.int32, (pairs, flat), 0)
    own = sub == me

    def down(x):
        top = jnp.max(x, axis=0, keepdims=True)
        return top + jnp.log(jnp.sum(jnp.exp(x - top), axis=0, keepdims=True))

    def across(x):
        top = jnp.max(x, axis=1, keepdims=True)
        total = jnp.sum(jnp.exp(x - top), axis=1, keepdims=True) * (1.0 / FOLD)
        return top + jnp.log(total)

    col_lse_all = down(scores)
    row_lse_all = down(scores_t)
    row = jnp.sum(jnp.where(own, scores, 0.0), axis=0, keepdims=True)
    col = jnp.sum(jnp.where(own, scores_t, 0.0), axis=0, keepdims=True)
    row_lse = across(row)
    col_lse = across(col)

    lane = lax.broadcasted_iota(jnp.int32, (1, flat), 1)
    row_mask = (lane >> 4) == pos
    col_mask = pos_of == me.astype(jnp.float32)
    single = lane == pos * FOLD
    loss = 0.5 * row_lse + jnp.sum(
        jnp.where(single, 0.5 * col_lse_all - row, 0.0), axis=1, keepdims=True
    )
    loss_ref[...] = jnp.broadcast_to(loss, loss_ref.shape)

    row_w = 0.5 * (jnp.exp(row - row_lse) + jnp.exp(row - col_lse_all)) - jnp.where(row_mask, 1.0, 0.0)
    col_w = 0.5 * (jnp.exp(col - row_lse_all) + jnp.exp(col - col_lse)) - jnp.where(col_mask, 1.0, 0.0)

    place = lax.broadcasted_iota(jnp.int32, (FOLD, flat), 0) == (
        lax.broadcasted_iota(jnp.int32, (FOLD, flat), 1) & (FOLD - 1)
    )

    def grad(weights, rows, out_ref):
        wide = jnp.where(place, jnp.broadcast_to(weights, place.shape), 0.0).astype(jnp.bfloat16)
        result = jnp.dot(wide, rows, preferred_element_type=jnp.float32)
        for c in range(FOLD):
            out_ref[0:1, c * width : (c + 1) * width] = result[c : c + 1, :]

    grad(row_w, passage, grad_q_ref)
    grad(col_w, query, grad_p_ref)


def kernel(
    subs, pairs,
    q_hbm, p_hbm, pos_hbm,
    grad_q_ref, grad_p_ref, loss_ref,
    same_place, block_ones, q_ref, p_ref, pos_ref, load_sem, ready, wide, both, places, send_sem, recv_sem, place_send, place_recv,
):
    width = both.shape[-1]
    chips = pairs // subs
    chip, sub = lax.axis_index("blk"), lax.axis_index("sub")
    me = chip * subs + sub
    other = (subs - 1) - sub

    def rows_to(target, source, k):
        return (
            pltpu.make_async_remote_copy(
                src_ref=both.at[source], dst_ref=both.at[source],
                send_sem=send_sem.at[k], recv_sem=recv_sem.at[source],
                device_id=target, device_id_type=MESH,
            ),
            pltpu.make_async_remote_copy(
                src_ref=places.at[source], dst_ref=places.at[source],
                send_sem=place_send.at[k], recv_sem=place_recv.at[source],
                device_id=target, device_id_type=MESH,
            ),
        )

    def over_link(k, source):
        return rows_to({"blk": k, "sub": sub}, source, k)

    def across(k):
        return rows_to({"blk": chip, "sub": other}, k * subs + sub, chips + k)

    def start(copies):
        for copy in copies:
            copy.start()

    def wait_recv(copies):
        for copy in copies:
            copy.wait_recv()

    def wait_send(copies):
        for copy in copies:
            copy.wait_send()

    def each(first, end, body):
        def step(k, carry):
            body(k)
            return carry

        lax.fori_loop(first, end, step, 0)

    q_copy = pltpu.make_async_copy(q_hbm, q_ref, load_sem.at[0])
    p_copy = pltpu.make_async_copy(p_hbm, p_ref, load_sem.at[1])
    pos_copy = pltpu.make_async_copy(pos_hbm, pos_ref, load_sem.at[2])
    pos_copy.start()
    q_copy.start()
    p_copy.start()

    barrier = pltpu.get_barrier_semaphore()

    def greet(k):
        pl.semaphore_signal(
            barrier, inc=1, device_id={"blk": k, "sub": sub}, device_id_type=MESH
        )

    each(chip + 1, chips, greet)
    pl.semaphore_signal(
        barrier, inc=1, device_id={"blk": chip, "sub": other}, device_id_type=MESH
    )

    pl.semaphore_wait(barrier, chip + 1)

    def tell(k):
        pl.semaphore_signal(
            ready.at[chip], inc=1, device_id={"blk": k, "sub": sub}, device_id_type=MESH
        )

    each(0, chip, tell)
    pos_copy.wait()
    pos = pos_ref[0]
    places[me] = jnp.full(places.shape[1:], pos.astype(jnp.float32), jnp.float32)
    q_copy.wait()
    p_copy.wait()
    for c in range(FOLD):
        wide[c : c + 1, :] = q_ref[0:1, c * width : (c + 1) * width]
        wide[FOLD + c : FOLD + c + 1, :] = p_ref[0:1, c * width : (c + 1) * width]
    both[me] = wide[...].astype(jnp.bfloat16)

    def send(k):
        start(over_link(k, me))

    def hand_on(k):
        wait_recv(over_link(k, k * subs + sub))
        start(across(k))

    def answer(k):
        pl.semaphore_wait(ready.at[k], 1)
        send(k)

    def receive(k):
        wait_recv(rows_to({"blk": chip, "sub": other}, k * subs + other, chips + k))

    each(0, chip, send)
    start(across(chip))
    each(chip + 1, chips, answer)
    flat = pairs * FOLD
    row_of = lax.broadcasted_iota(jnp.int32, (flat, flat), 0)
    lane_of = lax.broadcasted_iota(jnp.int32, (flat, flat), 1)
    same_place[...] = jnp.where((row_of & (FOLD - 1)) == (lane_of & (FOLD - 1)), 1.0, 0.0)
    block_ones[...] = jnp.where((row_of >> 4) == (lane_of >> 4), 1.0, 0.0).astype(jnp.bfloat16)
    each(0, chip, hand_on)
    each(chip + 1, chips, hand_on)
    each(0, chips, receive)

    lane = lax.broadcasted_iota(jnp.int32, (1, pairs * FOLD), 1)
    pos_of = jnp.zeros((1, pairs * FOLD), jnp.float32)
    for k in range(pairs):
        pos_of = jnp.where((lane >> 4) == k, places[k, 0:1, :], pos_of)

    finish(pairs, me, same_place, block_ones, both[...], pos, pos_of, loss_ref, grad_q_ref, grad_p_ref)

    each(0, chip, lambda k: wait_send(over_link(k, me)))
    each(chip + 1, chips, lambda k: wait_send(over_link(k, me)))
    each(0, chips, lambda k: wait_send(across(k)))


def write_out(loss_ref, q_ref, p_ref, loss_out, q_out, p_out):
    loss_out[...] = loss_ref[0, 0:1]
    q_out[...] = score_scale * q_ref[...]
    p_out[...] = score_scale * p_ref[...]


def local(subs, pairs, queries, passages, positive):
    width = queries.shape[1] // FOLD
    vmem = pl.BlockSpec(memory_space=pltpu.VMEM)
    anywhere = pl.BlockSpec(memory_space=pltpu.HBM)
    flat = pairs * FOLD
    grad_q, grad_p, loss = pl.pallas_call(
        functools.partial(kernel, subs, pairs),
        out_shape=(
            pltpu.VMEM(queries.shape, jnp.float32),
            pltpu.VMEM(passages.shape, jnp.float32),
            pltpu.VMEM((1, 128), jnp.float32),
        ),
        in_specs=[anywhere, anywhere, anywhere],
        out_specs=(vmem, vmem, vmem),
        scratch_shapes=[
            pltpu.VMEM((flat, flat), jnp.float32),
            pltpu.VMEM((flat, flat), jnp.bfloat16),
            pltpu.VMEM(queries.shape, jnp.float32),
            pltpu.VMEM(passages.shape, jnp.float32),
            pltpu.SMEM((1,), jnp.int32),
            pltpu.SemaphoreType.DMA((3,)),
            pltpu.SemaphoreType.REGULAR((pairs // subs,)),
            pltpu.VMEM((2 * FOLD, width), jnp.float32),
            pltpu.VMEM((pairs, 2 * FOLD, width), jnp.bfloat16),
            pltpu.VMEM((pairs, 1, flat), jnp.float32),
            pltpu.SemaphoreType.DMA((pairs,)),
            pltpu.SemaphoreType.DMA((pairs,)),
            pltpu.SemaphoreType.DMA((pairs,)),
            pltpu.SemaphoreType.DMA((pairs,)),
        ],
        compiler_params=pltpu.CompilerParams(collective_id=0, has_side_effects=True, vmem_limit_bytes=8 * 1024 * 1024),
    )(*(pltpu.with_memory_space_constraint(x, pltpu.HBM) for x in (queries, passages)), positive)
    return pl.pallas_call(
        write_out,
        out_shape=(
            jax.ShapeDtypeStruct((1,), jnp.float32),
            jax.ShapeDtypeStruct(queries.shape, jnp.float32),
            jax.ShapeDtypeStruct(passages.shape, jnp.float32),
        ),
        in_specs=[vmem, vmem, vmem],
        out_specs=(vmem, vmem, vmem),
        compiler_params=pltpu.CompilerParams(vmem_limit_bytes=8 * 1024 * 1024),
    )(loss, grad_q, grad_p)


def solution(mesh):
    in_specs = (
        P(("rep", "blk", "sub"), None),
        P(("rep", "blk", "sub"), None),
        P(("rep", "blk", "sub")),
    )
    out_specs = (
        P(("rep", "blk", "sub")),
        P(("rep", "blk", "sub"), None),
        P(("rep", "blk", "sub"), None),
    )
    subs = mesh.shape["sub"]
    group = mesh.shape["blk"] * subs

    def run(queries, passages, positive):
        if queries.shape[0] == 1 and subs == 2 and group * FOLD <= 256:
            return local(subs, group, queries, passages, positive)
        return spread(queries, passages, positive)

    return jax.shard_map(run, mesh=mesh, in_specs=in_specs, out_specs=out_specs, check_vma=False)
```
